1024 devices in a mesh: group: 8 (over y), local: 128 (over z, x, core).
Axes of the slice: x: 4, y: 8, z: 16, core: 2. Of those that a mesh axis runs over, the one named last changes fastest.
Arguments:
- grad_out: bfloat16 [4096, 7168], P('group', 'local'), may hold values from -6 to 6
- tokens_in: bfloat16 [4096, 7168], P('group', 'local'), may hold values from -6 to 6
- expert_ids: int32 [4096, 8], P('group'), may hold values from 0 to 255, as said below
- gate_values: float32 [4096, 8], P('group'), may hold values from 0.05 to 0.6
- w_gate: bfloat16 [8, 128, 448, 256], P('group', 'local'), may hold values from -0.0625 to 0.0625
- w_up: bfloat16 [8, 128, 448, 256], P('group', 'local'), may hold values from -0.0625 to 0.0625
- w_down_t: bfloat16 [8, 128, 448, 256], P('group', 'local'), may hold values from -0.125 to 0.125
Outputs:
- grad_tokens: bfloat16 [4096, 7168], P('group', 'local')
- grad_gate: float32 [8, 128, 448, 256], P('group', 'local')
- grad_up: float32 [8, 128, 448, 256], P('group', 'local')
- grad_down_t: float32 [8, 128, 448, 256], P('group', 'local')
The draws below stay inside these ranges and needn't reach their ends.
Inputs may be any that keep to these rules, and one draw needn't show every extreme that they name: `expert_ids`: each token names 8 different experts, all from at most 4 groups (expert e belongs to group e // 32), and at most one first expert of a group. Of the 512 tokens of one group at most 32 name the first expert of any one group; this number is reached for some group from the tokens of every group, and for one group from the tokens of all groups.
All inputs are finite; a program needn't handle non-finite values.
Results may differ from the reference program's by a relative error of at most 0.0057.
Values may be sent and summed in bfloat16 or wider, within the bound.
A program may use at most 32 MiB of HBM per device.

```python
import jax
import jax.numpy as jnp
from jax import lax

D = 7168
H = 2048
EXP_GRP = 32
TOPK = 8
TOPG = 4
TOK_GRP = 512
CAP = 32
TOKENS = 4096
DSPLIT = 16
HBLK = 8
DQ = 448
HS = 256
N_GROUP = 8
N_LOCAL = 128


def draw_expert_ids(key, part):
    key = jax.random.fold_in(key, 7)
    keys = jax.random.split(key, 8)
    dest = jnp.arange(N_GROUP, dtype=jnp.int32)
    counts = jax.random.randint(keys[0], (N_GROUP, N_GROUP), CAP // 4, CAP + 1)
    full_all = jax.random.randint(keys[1], (), 0, N_GROUP)
    full_own = jax.random.randint(keys[2], (N_GROUP,), 0, N_GROUP)
    counts = jnp.where(dest[None, :] == full_all, CAP, counts)
    counts = jnp.where(dest[None, :] == full_own[:, None], CAP, counts)
    perm_keys = jax.random.split(keys[3], N_GROUP)
    places = jax.vmap(lambda each_key: jax.random.permutation(each_key, TOK_GRP))(perm_keys)
    lower = dest * CAP
    inside = (places[:, :, None] >= lower[None, None, :]) & (places[:, :, None] < lower[None, None, :] + counts[:, None, :])
    named = jnp.any(inside, axis=-1).reshape(-1)
    window = jnp.sum(inside.astype(jnp.int32) * dest[None, None, :], axis=-1).reshape(-1)
    row_count = N_GROUP * TOK_GRP
    scores = jax.random.randint(keys[4], (row_count, N_GROUP), 0, 1024) * N_GROUP + dest[None, :]
    top_score = 1024 * N_GROUP + N_GROUP
    scores = jnp.where(named[:, None] & (dest[None, :] == window[:, None]), top_score, scores)
    chosen = lax.top_k(scores, TOPG)[1].astype(jnp.int32)
    first = jax.random.randint(keys[5], (row_count, TOPG), 1, EXP_GRP)
    stride = jax.random.randint(keys[6], (row_count, TOPG), 1, EXP_GRP - 1)
    second = 1 + (first - 1 + stride) % (EXP_GRP - 1)
    local_ids = jnp.stack([first, second], axis=-1)
    expert_ids = (chosen[:, :, None] * EXP_GRP + local_ids).reshape(row_count, TOPK)
    expert_ids = expert_ids.at[:, 0].set(jnp.where(named, window * EXP_GRP, expert_ids[:, 0]))
    order_keys = jax.random.randint(keys[7], (row_count, TOPK), 0, 64) * TOPK + jnp.arange(TOPK, dtype=jnp.int32)[None, :]
    order = jnp.argsort(order_keys, axis=-1, stable=True)
    return jnp.take_along_axis(expert_ids, order, axis=-1).astype(jnp.int32)


def shard_levels(rng, shape, pieces, low, top_value):
    factor_of, own = 1.0, jax.random.fold_in(rng, 6)
    for dim, shards_of in pieces:
        steps = jnp.exp(jax.random.uniform(jax.random.fold_in(own, dim), (shards_of,), jnp.float32, low / len(pieces), top_value / len(pieces)))
        factor_of = factor_of * jnp.repeat(steps, shape[dim] // shards_of).reshape([-1 if axis == dim else 1 for axis in range(len(shape))])
    return factor_of


def scatter_about(key, shape, deviation, limit, cuts=(), held_as=jnp.bfloat16):
    array = jax.random.normal(key, shape, jnp.float32) * deviation
    if len(cuts) > 0:
        array = shard_levels(key, shape, cuts, -0.22, 0.18) * array
    return jnp.clip(array, min=-limit, max=limit).astype(held_as)


def setup_inputs(seed: int = 0) -> dict:
    arg_keys = jax.random.split(jax.random.key(seed), 8)
    return {
        "grad_out": scatter_about(arg_keys[0], (TOKENS, D), 1.0, 6.0, ((0, 8), (1, 128))),
        "tokens_in": scatter_about(arg_keys[1], (TOKENS, D), 1.0, 6.0, ((0, 8), (1, 128))),
        "expert_ids": draw_expert_ids(jax.random.fold_in(arg_keys[7], 71), 0),
        "gate_values": jnp.clip(0.05 + 0.55 * jax.random.uniform(arg_keys[3], (TOKENS, TOPK), jnp.float32) ** shard_levels(arg_keys[3], (TOKENS, TOPK), ((0, 8),), -0.2, 0.2), 0.05, 0.6),
        "w_gate": scatter_about(arg_keys[4], (N_GROUP, N_LOCAL, DQ, HS), D ** -0.5, 0.0625, ((0, 8), (1, 128))),
        "w_up": scatter_about(arg_keys[5], (N_GROUP, N_LOCAL, DQ, HS), D ** -0.5, 0.0625, ((0, 8), (1, 128))),
        "w_down_t": scatter_about(arg_keys[6], (N_GROUP, N_LOCAL, DQ, HS), H ** -0.5, 0.125, ((0, 8), (1, 128))),
    }


def to_full(blocks):
    return blocks.reshape(N_GROUP, DSPLIT, HBLK, DQ, HS).transpose(0, 1, 3, 2, 4).reshape(N_GROUP, D, H)


def to_blocks(full):
    return full.reshape(N_GROUP, DSPLIT, DQ, HBLK, HS).transpose(0, 1, 3, 2, 4).reshape(N_GROUP, N_LOCAL, DQ, HS)


def gate_backward(pre_gate, pre_up, grad_hidden):
    sigma = jax.nn.sigmoid(pre_gate)
    hidden = (pre_gate * sigma * pre_up).astype(jnp.bfloat16)
    d_gate = (grad_hidden * pre_up * sigma * (1.0 + pre_gate * (1.0 - sigma))).astype(jnp.bfloat16)
    d_up = (grad_hidden * pre_gate * sigma).astype(jnp.bfloat16)
    return d_gate, d_up, hidden


def reference(grad_out, tokens_in, expert_ids, gate_values, w_gate, w_up, w_down_t):
    full_gate = to_full(w_gate)
    full_up = to_full(w_up)
    full_down = to_full(w_down_t)
    slot_count = N_GROUP * CAP

    def one_expert(inputs):
        group_id, gate_mat, up_mat, down_mat = inputs
        matches = expert_ids == group_id * EXP_GRP
        hit_mask = jnp.any(matches, axis=1)
        gate_row = jnp.sum(jnp.where(matches, gate_values, jnp.float32(0.0)), axis=1)
        slot_rows = jnp.nonzero(hit_mask, size=slot_count, fill_value=0)[0].astype(jnp.int32)
        valid = jnp.arange(slot_count, dtype=jnp.int32) < jnp.sum(hit_mask.astype(jnp.int32))
        x_rows = jnp.where(valid[:, None], tokens_in[slot_rows], jnp.zeros((), jnp.bfloat16))
        scaled = (gate_row[slot_rows][:, None] * grad_out[slot_rows].astype(jnp.float32)).astype(jnp.bfloat16)
        scaled = jnp.where(valid[:, None], scaled, jnp.zeros((), jnp.bfloat16))
        pre_gate = jnp.dot(x_rows, gate_mat, preferred_element_type=jnp.float32)
        pre_up = jnp.dot(x_rows, up_mat, preferred_element_type=jnp.float32)
        grad_hidden = jnp.dot(scaled, down_mat, preferred_element_type=jnp.float32)
        d_gate, d_up, hidden = gate_backward(pre_gate, pre_up, grad_hidden)
        contrib = jnp.dot(d_gate, gate_mat.T, preferred_element_type=jnp.float32)
        contrib = contrib + jnp.dot(d_up, up_mat.T, preferred_element_type=jnp.float32)
        contrib = jnp.where(valid[:, None], contrib, jnp.float32(0.0))
        grad_g = jnp.dot(x_rows.T, d_gate, preferred_element_type=jnp.float32)
        grad_u = jnp.dot(x_rows.T, d_up, preferred_element_type=jnp.float32)
        grad_d = jnp.dot(scaled.T, hidden, preferred_element_type=jnp.float32)
        return slot_rows, contrib, grad_g, grad_u, grad_d

    group_ids = jnp.arange(N_GROUP, dtype=jnp.int32)
    slot_rows, contribs, grad_g, grad_u, grad_d = lax.map(one_expert, (group_ids, full_gate, full_up, full_down))
    grad_tokens = jnp.zeros((TOKENS, D), jnp.float32).at[slot_rows.reshape(-1)].add(contribs.reshape(-1, D))
    return grad_tokens.astype(jnp.bfloat16), to_blocks(grad_g), to_blocks(grad_u), to_blocks(grad_d)
```

```python
import jax
import jax.numpy as jnp
from jax import lax
from jax.experimental import pallas as pl
from jax.experimental.pallas import tpu as pltpu
from jax.sharding import PartitionSpec as P

EXP_GRP = 32
CAP = 32
NY = 8
NZ = 16
NX = 4
TOK = 512
COLS = 56
FEAT = 448
HID = 256
HALF = 2
ROWS = NY * CAP // HALF
PIECE = CAP // HALF
LANES = 128
MESH = pl.DeviceIdType.MESH
BF16 = jnp.bfloat16
F32 = jnp.float32
FAR_FIRST = (8, 7, 9, 6, 10, 5, 11, 4, 12, 3, 13, 2, 14, 1, 15)
Y_ORDER = (4, 3, 5, 2, 6, 1, 7)
X_ORDER = (1, 3, 2)


def dot(left, right):
    return jnp.dot(left, right, preferred_element_type=F32)


def dot_nt(left, right):
    return lax.dot_general(left, right, (((1,), (1,)), ((), ())), preferred_element_type=F32)


def kernel(
    dy_hbm, x_hbm, ids_hbm, gate_hbm, wg_hbm, wu_hbm, wd_hbm,
    tok_out, og_hbm, ou_hbm, od_hbm,
    dy, xin, ids, gates, wg, wu, wd,
    sel, sel_t, snd, rows, wp_gu, wp_d, part_f, part_b, part_r, hid_r, rows_t,
    dgu, hid, ret, ret_sib, ret_sum, ret_x, home_s, home_r, tok, og, ou, od,
    in_sem, out_sem, y_s, y_r, x_s, x_r, c_s, c_r, rs_s, rs_r, ag_s, ag_r,
    e1_s, e1_r, e2_s, e2_r, f_s, f_r,
):
    y = lax.axis_index("group")
    l = lax.axis_index("local")
    z = l // 8
    j = lax.rem(l, 8)
    x = j // 2
    c = lax.rem(j, 2)

    def at_y(d):
        return (lax.rem(y + d, NY), l)

    def at_z(d):
        return (y, lax.rem(z + d, NZ) * 8 + j)

    def at_x(d):
        return (y, z * 8 + lax.rem(x + d, NX) * 2 + c)

    sib = (y, z * 8 + x * 2 + 1 - c)

    barrier = pltpu.get_barrier_semaphore()
    partners = (
        [at_z(d) for d in FAR_FIRST] + [at_y(d) for d in Y_ORDER] + [at_x(d) for d in X_ORDER] + [sib]
    )
    for who in partners:
        pl.semaphore_signal(barrier, inc=1, device_id=who, device_id_type=MESH)

    loads = [
        pltpu.make_async_copy(src, dst, in_sem.at[num])
        for num, (src, dst) in enumerate(
            (
                (ids_hbm, ids),
                (gate_hbm, gates),
                (x_hbm, xin),
                (dy_hbm, dy),
                (wg_hbm.at[0, 0], wg),
                (wu_hbm.at[0, 0], wu),
                (wd_hbm.at[0, 0], wd),
            )
        )
    ]
    for load in loads:
        load.start()

    def send(src, dst, send_sem, recv_sem, who):
        copy = pltpu.make_async_remote_copy(
            src_ref=src, dst_ref=dst, send_sem=send_sem, recv_sem=recv_sem,
            device_id=who, device_id_type=MESH,
        )
        copy.start()
        return copy

    loads[0].wait()
    loads[1].wait()
    fill = jnp.zeros((TOK, LANES - 8), F32)
    ids_t = jnp.concatenate([ids[...].astype(F32), fill], axis=1).T[:8]
    gates_t = jnp.concatenate([gates[...], fill], axis=1).T[:8]
    target = (lax.broadcasted_iota(jnp.int32, (NY, TOK), 0) * EXP_GRP).astype(F32)
    hit = jnp.zeros((NY, TOK), F32)
    gate_of = jnp.zeros((NY, TOK), F32)
    for k in range(8):
        same = jnp.broadcast_to(ids_t[k : k + 1], (NY, TOK)) == target
        hit = jnp.where(same, 1.0, hit)
        gate_of = gate_of + jnp.where(same, jnp.broadcast_to(gates_t[k : k + 1], (NY, TOK)), 0.0)
    before = (
        lax.broadcasted_iota(jnp.int32, (TOK, TOK), 0) < lax.broadcasted_iota(jnp.int32, (TOK, TOK), 1)
    )
    rank = dot(hit.astype(BF16), jnp.where(before, 1.0, 0.0).astype(BF16))
    rank = jnp.where(hit > 0.0, rank, -1.0)
    loads[2].wait()
    loads[3].wait()
    gap = jnp.zeros((TOK, LANES // 2 - COLS), BF16)
    pair = jnp.concatenate([xin[...], gap, dy[...], gap], axis=1)
    upper = lax.broadcasted_iota(jnp.int32, (ROWS, LANES), 1) >= LANES // 2
    rank_b = jnp.broadcast_to(rank[:, None, :], (NY, PIECE, TOK)).reshape(ROWS, TOK)
    gate_b = jnp.broadcast_to(gate_of[:, None, :], (NY, PIECE, TOK)).reshape(ROWS, TOK)
    slot = lax.rem(lax.broadcasted_iota(jnp.int32, (ROWS, TOK), 0), PIECE).astype(F32)
    for h in range(HALF):
        chosen = rank_b == slot + float(h * PIECE)
        one_hot = jnp.where(chosen, 1.0, 0.0).astype(BF16)
        sel[h * ROWS : (h + 1) * ROWS, :] = one_hot
        slot_gate = jnp.sum(jnp.where(chosen, gate_b, 0.0), axis=1, keepdims=True)
        picked = dot(one_hot, pair)
        picked = jnp.where(upper, slot_gate * picked, picked)
        snd[h] = picked.astype(BF16).reshape(NY, PIECE, LANES)

    pl.semaphore_wait(barrier, len(partners))

    waits = []
    y_copies = [
        send(snd.at[:, lax.rem(y + d, NY)], rows.at[:, j, y], y_s.at[d - 1], y_r.at[d - 1], at_y(d))
        for d in Y_ORDER
    ]
    for h in range(HALF):
        rows[h, j, y] = snd[h, y]

    for load in loads[4:]:
        load.wait()
    zero_rows = jnp.zeros((LANES // 2 - COLS, HID), F32)

    def block(ref, num):
        first = num * COLS
        skip = first % 16
        return jnp.concatenate(
            [ref[first - skip : first + COLS, :].astype(F32)[skip:], zero_rows], axis=0
        ).astype(BF16)

    h0, h1 = slice(0, LANES), slice(LANES, HID)
    for num in range(8):
        low = slice(num * LANES, num * LANES + LANES // 2)
        high = slice(num * LANES + LANES // 2, (num + 1) * LANES)
        g_blk, u_blk, d_blk = block(wg, num), block(wu, num), block(wd, num)
        wp_gu[low, :] = jnp.concatenate([g_blk[:, h0], u_blk[:, h0], g_blk[:, h1], u_blk[:, h1]], axis=1)
        wp_gu[high, :] = jnp.zeros((LANES // 2, 2 * HID), BF16)
        wp_d[low, :] = jnp.zeros((LANES // 2, HID), BF16)
        wp_d[high, :] = d_blk

    for copy in y_copies:
        copy.wait_recv()
    waits += y_copies

    x_copies = []
    c_copies = []
    for h in range(HALF):
        mine = rows.at[h, j]
        x_copies.append({
            d: send(mine, mine, x_s.at[h, d - 1], x_r.at[h, d - 1], at_x(d)) for d in X_ORDER
        })
        c_copies.append({0: send(mine, mine, c_s.at[h, 0], c_r.at[h, 0], sib)})

    rs_copies = []
    for h in range(HALF):
        for d in X_ORDER:
            x_copies[h][d].wait_recv()
            piece = rows.at[h, lax.rem(x + NX - d, NX) * 2 + c]
            c_copies[h][d] = send(piece, piece, c_s.at[h, d], c_r.at[h, d], sib)
        acc_gu = jnp.zeros((ROWS, 2 * HID), F32)
        acc_d = jnp.zeros((ROWS, HID), F32)
        for d in (0,) + X_ORDER:
            c_copies[h][d].wait_recv()
            chip = lax.rem(x + NX - d, NX)
            lhs = jnp.concatenate(
                [rows[h, chip * 2].reshape(ROWS, LANES), rows[h, chip * 2 + 1].reshape(ROWS, LANES)], axis=1
            )
            span = pl.ds(pl.multiple_of(chip * 2 * LANES, 2 * LANES), 2 * LANES)
            acc_gu = acc_gu + dot(lhs, wp_gu[span, :])
            acc_d = acc_d + dot(lhs, wp_d[span, :])
        lo = jnp.concatenate([acc_gu[:, :HID], acc_d[:, :LANES]], axis=1).reshape(NZ, 8, 3 * LANES)
        hi = jnp.concatenate([acc_gu[:, HID:], acc_d[:, LANES:]], axis=1).reshape(NZ, 8, 3 * LANES)
        both = jnp.concatenate([lo, hi], axis=1)
        part_f[h] = both
        part_b[h] = both.astype(BF16)
        rs_copies.append([
            send(part_b.at[h, lax.rem(z + d, NZ)], part_r.at[h, num], rs_s.at[h, num], rs_r.at[h, num], at_z(d))
            for num, d in enumerate(FAR_FIRST)
        ])
        waits += list(x_copies[h].values()) + list(c_copies[h].values())

    sel_t[...] = sel[...].T
    for h in range(HALF):
        for num in range(8):
            rows_t[num * LANES : (num + 1) * LANES, h * ROWS : (h + 1) * ROWS] = (
                rows[h, num].reshape(ROWS, LANES).T
            )

    ag_copies = []
    for h in range(HALF):
        total = part_f[h, z]
        for num in range(NZ - 1):
            rs_copies[h][num].wait_recv()
            total = total + part_r[h, num].astype(F32)
        pre_gate = total[:, :LANES]
        pre_up = total[:, LANES : 2 * LANES]
        back = total[:, 2 * LANES :]
        sigma = 1.0 / (1.0 + jnp.exp(-pre_gate))
        hidden = pre_gate * sigma * pre_up
        d_gate = back * pre_up * sigma * (1.0 + pre_gate * (1.0 - sigma))
        d_up = back * pre_gate * sigma
        hid_r[h, z] = jnp.concatenate([d_gate, d_up, hidden], axis=1).astype(BF16)
        mine = hid_r.at[h, z]
        ag_copies.append([
            send(mine, mine, ag_s.at[h, num], ag_r.at[h, num], at_z(d)) for num, d in enumerate(FAR_FIRST)
        ])
        waits += rs_copies[h]

    low_lane = lax.broadcasted_iota(jnp.int32, (ROWS // 2, LANES), 1) < LANES // 2
    e1_copies = []
    e2_copies = []

    def sum_cores(h):
        e1_copies[h].wait_recv()
        for chip in range(NX):
            ret_sum[h, chip] = ret[h, chip, c] + ret_sib[h, chip]
        e2_copies.append([
            send(ret_sum.at[h, lax.rem(x + d, NX)], ret_x.at[h, d - 1], e2_s.at[h, d - 1], e2_r.at[h, d - 1], at_x(d))
            for d in X_ORDER
        ])

    for h in range(HALF):
        for copy in ag_copies[h]:
            copy.wait_recv()
        waits += ag_copies[h]
        got = hid_r[h].astype(F32)
        lo = got[:, :8].reshape(ROWS, 3 * LANES)
        hi = got[:, 8:].reshape(ROWS, 3 * LANES)
        d_gu = jnp.concatenate([lo[:, :HID], hi[:, :HID]], axis=1).astype(BF16)
        span = slice(h * ROWS, (h + 1) * ROWS)
        dgu[span, :] = d_gu
        hid[span, :] = jnp.concatenate([lo[:, HID:], hi[:, HID:]], axis=1).astype(BF16)
        for num in range(8):
            out = dot_nt(d_gu, wp_gu[num * LANES : (num + 1) * LANES, :])
            ret[h, num // 2, num % 2] = jnp.where(
                low_lane, out[: ROWS // 2], pltpu.roll(out[ROWS // 2 :], LANES // 2, 1)
            )
        e1_copies.append(send(ret.at[h, :, 1 - c], ret_sib.at[h], e1_s.at[h], e1_r.at[h], sib))
        if h == 0:
            sum_cores(0)
    sum_cores(1)
    waits += e1_copies

    gu_all = dgu[...]
    hid_all = hid[...]
    for num in range(8):
        low = slice(num * LANES, num * LANES + LANES // 2)
        high = slice(num * LANES + LANES // 2, (num + 1) * LANES)
        to = slice(num * COLS, (num + 1) * COLS)
        both = dot(rows_t[low, :], gu_all)[:COLS]
        og[to, h0] = both[:, :LANES]
        ou[to, h0] = both[:, LANES:HID]
        og[to, h1] = both[:, HID : HID + LANES]
        ou[to, h1] = both[:, HID + LANES :]
        od[to, :] = dot(rows_t[high, :], hid_all)[:COLS]
    stores = [
        pltpu.make_async_copy(src, dst.at[0, 0], out_sem.at[num])
        for num, (src, dst) in enumerate(((og, og_hbm), (ou, ou_hbm), (od, od_hbm)))
    ]
    for store in stores:
        store.start()

    ends = []
    for h in range(HALF):
        total = ret_sum[h, x]
        for d in X_ORDER:
            e2_copies[h][X_ORDER.index(d)].wait_recv()
            total = total + ret_x[h, d - 1]
        ends.append(total)
        waits += e2_copies[h]
    first = jnp.where(low_lane, ends[0], pltpu.roll(ends[1], LANES // 2, 1))
    second = jnp.where(low_lane, pltpu.roll(ends[0], LANES // 2, 1), ends[1])
    home_s[: NY // 2] = first.astype(BF16).reshape(NY // 2, PIECE, LANES)
    home_s[NY // 2 :] = second.astype(BF16).reshape(NY // 2, PIECE, LANES)
    f_copies = [
        send(home_s.at[lax.rem(y + d, NY)], home_r.at[y], f_s.at[d - 1], f_r.at[d - 1], at_y(d))
        for d in Y_ORDER
    ]
    home_r[y] = home_s[y]
    for copy in waits:
        copy.wait_send()
    for copy in f_copies:
        copy.wait_recv()
    home = home_r[...].reshape(ROWS, LANES)
    both = jnp.concatenate([home.astype(F32), pltpu.roll(home.astype(F32), LANES // 2, 1)], axis=0).astype(BF16)
    tok[...] = dot(sel_t[...], both)[:, :COLS].astype(BF16)
    last = pltpu.make_async_copy(tok, tok_out, out_sem.at[3])
    last.start()
    for copy in f_copies:
        copy.wait_send()
    for store in stores:
        store.wait()
    last.wait()


def per_device(grad_out, tokens_in, expert_ids, gate_values, w_gate, w_up, w_down_t):
    vm = pltpu.VMEM
    dma = pltpu.SemaphoreType.DMA
    scratch = [
        vm((TOK, COLS), BF16), vm((TOK, COLS), BF16), vm((TOK, 8), jnp.int32), vm((TOK, 8), F32),
        vm((FEAT, HID), BF16), vm((FEAT, HID), BF16), vm((FEAT, HID), BF16),
        vm((HALF * ROWS, TOK), BF16),
        vm((TOK, HALF * ROWS), BF16),
        vm((HALF, NY, PIECE, LANES), BF16),
        vm((HALF, 8, NY, PIECE, LANES), BF16),
        vm((8 * LANES, 2 * HID), BF16),
        vm((8 * LANES, HID), BF16),
        vm((HALF, NZ, 16, 3 * LANES), F32),
        vm((HALF, NZ, 16, 3 * LANES), BF16),
        vm((HALF, NZ - 1, 16, 3 * LANES), BF16),
        vm((HALF, NZ, 16, 3 * LANES), BF16),
        vm((8 * LANES, HALF * ROWS), BF16),
        vm((HALF * ROWS, 2 * HID), BF16),
        vm((HALF * ROWS, HID), BF16),
        vm((HALF, NX, 2, ROWS // 2, LANES), F32),
        vm((HALF, NX, ROWS // 2, LANES), F32),
        vm((HALF, NX, ROWS // 2, LANES), F32),
        vm((HALF, NX - 1, ROWS // 2, LANES), F32),
        vm((NY, PIECE, LANES), BF16),
        vm((NY, PIECE, LANES), BF16),
        vm((TOK, COLS), BF16),
        vm((FEAT, HID), F32), vm((FEAT, HID), F32), vm((FEAT, HID), F32),
        dma((7,)), dma((4,)),
        dma((NY - 1,)), dma((NY - 1,)),
        dma((HALF, NX - 1)), dma((HALF, NX - 1)),
        dma((HALF, NX)), dma((HALF, NX)),
        dma((HALF, NZ - 1)), dma((HALF, NZ - 1)),
        dma((HALF, NZ - 1)), dma((HALF, NZ - 1)),
        dma((HALF,)), dma((HALF,)),
        dma((HALF, NX - 1)), dma((HALF, NX - 1)),
        dma((NY - 1,)), dma((NY - 1,)),
    ]
    grad = jax.ShapeDtypeStruct((1, 1, FEAT, HID), F32)
    return pl.pallas_call(
        kernel,
        name="expert_backward",
        out_shape=(jax.ShapeDtypeStruct((TOK, COLS), BF16), grad, grad, grad),
        in_specs=[pl.BlockSpec(memory_space=pl.ANY)] * 7,
        out_specs=[pl.BlockSpec(memory_space=pl.ANY)] * 4,
        scratch_shapes=scratch,
        compiler_params=pltpu.CompilerParams(
            collective_id=0, has_side_effects=True, vmem_limit_bytes=48 << 20
        ),
    )(grad_out, tokens_in, expert_ids, gate_values, w_gate, w_up, w_down_t)


def solution(mesh):
    placed = (
        P("group", "local"),
        P("group", "local"),
        P("group", None),
        P("group", None),
        P("group", "local", None, None),
        P("group", "local", None, None),
        P("group", "local", None, None),
    )
    return jax.shard_map(
        per_device,
        mesh=mesh,
        in_specs=placed,
        out_specs=(
            P("group", "local"),
            P("group", "local", None, None),
            P("group", "local", None, None),
            P("group", "local", None, None),
        ),
        check_vma=False,
    )
```

```python
import jax
import jax.numpy as jnp
from jax import lax
from jax.experimental import pallas as pl
from jax.experimental.pallas import tpu as pltpu
from jax.sharding import PartitionSpec as P

EXP_GRP = 32
CAP = 32
NY = 8
NZ = 16
NX = 4
TOK = 512
COLS = 56
FEAT = 448
HID = 256
HALF = 2
ROWS = NY * CAP // HALF
PIECE = CAP // HALF
LANES = 128
MESH = pl.DeviceIdType.MESH
VMEM_FOR_KERNEL = (64 << 20) - 1441792
BF16 = jnp.bfloat16
F32 = jnp.float32
QUAD = 4
FAR = (8, 4, 12)
AHEAD = (2, 1, 3, 0)
NEAR = ((2, 1, 15), (14, 1, 15))
Z_BESIDE = (2, 14, 1, 15)
Y_ORDER = (4, 3, 5, 2, 6, 1, 7)
X_ORDER = (1, 3, 2)


def dot(left, right):
    return jnp.dot(left, right, preferred_element_type=F32)


def dot_nt(left, right):
    return lax.dot_general(left, right, (((1,), (1,)), ((), ())), preferred_element_type=F32)


def kernel(
    dy_hbm, x_hbm, ids_hbm, gate_hbm, wg_hbm, wu_hbm, wd_hbm,
    tok_out, og_hbm, ou_hbm, od_hbm,
    dy, xin, ids, gates, wg, wu, wd,
    sel, snd, rows, wp_gu, wp_d, part_f, part_b, near_r, quad_b, far_r, hid_r, rows_t,
    dgu, hid, ret, ret_sib, ret_sum, ret_send, ret_x, home_s, home_r, tok, og, ou, od,
    in_sem, out_sem, y_s, y_r, x_s, x_r, c_s, c_r, rn_s, rn_r, rf_s, rf_r, gf_s, gf_r, gn_s, gn_r,
    e1_s, e1_r, e2_s, e2_r, f_s, f_r, by_two, by_four,
):
    y = lax.axis_index("group")
    l = lax.axis_index("local")
    z = l // 8
    q = lax.rem(z, QUAD)
    m = z // QUAD
    j = lax.rem(l, 8)
    x = j // 2
    c = lax.rem(j, 2)

    def at_y(d):
        return (lax.rem(y + d, NY), l)

    def at_z(d):
        return (y, lax.rem(z + d, NZ) * 8 + j)

    def at_x(d):
        return (y, z * 8 + lax.rem(x + d, NX) * 2 + c)

    sib = (y, z * 8 + x * 2 + 1 - c)

    barrier = pltpu.get_barrier_semaphore()
    partners = (
        [at_z(d) for d in Z_BESIDE] + [at_y(d) for d in Y_ORDER] + [at_x(d) for d in X_ORDER] + [sib]
    )
    for who in partners:
        pl.semaphore_signal(barrier, inc=1, device_id=who, device_id_type=MESH)

    loads = [
        pltpu.make_async_copy(src, dst, in_sem.at[num])
        for num, (src, dst) in enumerate(
            (
                (ids_hbm, ids),
                (gate_hbm, gates),
                (x_hbm, xin),
                (dy_hbm, dy),
                (wg_hbm.at[0, 0], wg),
                (wu_hbm.at[0, 0], wu),
                (wd_hbm.at[0, 0], wd),
            )
        )
    ]
    for load in loads:
        load.start()

    def send(src, dst, send_sem, recv_sem, who):
        copy = pltpu.make_async_remote_copy(
            src_ref=src, dst_ref=dst, send_sem=send_sem, recv_sem=recv_sem,
            device_id=who, device_id_type=MESH,
        )
        copy.start()
        return copy

    loads[0].wait()
    loads[1].wait()
    ids_t = ids[...]
    gates_t = gates[...]
    target = lax.broadcasted_iota(jnp.int32, (NY, TOK), 0) * EXP_GRP
    hit = jnp.zeros((NY, TOK), F32)
    gate_of = jnp.zeros((NY, TOK), F32)
    for k in range(8):
        same = jnp.broadcast_to(ids_t[k : k + 1], (NY, TOK)) == target
        hit = jnp.where(same, 1.0, hit)
        gate_of = gate_of + jnp.where(same, jnp.broadcast_to(gates_t[k : k + 1], (NY, TOK)), 0.0)
    before = (
        lax.broadcasted_iota(jnp.int32, (TOK, TOK), 0) < lax.broadcasted_iota(jnp.int32, (TOK, TOK), 1)
    )
    rank = dot(hit.astype(BF16), jnp.where(before, 1.0, 0.0).astype(BF16))
    rank = jnp.where(hit > 0.0, rank, -1.0)
    loads[2].wait()
    loads[3].wait()
    gap = jnp.zeros((LANES // 2 - COLS, TOK), F32)
    pair = jnp.concatenate([xin[...].astype(F32), gap, dy[...].astype(F32), gap], axis=0).astype(BF16)
    upper = lax.broadcasted_iota(jnp.int32, (ROWS, LANES), 1) >= LANES // 2
    rank_b = jnp.broadcast_to(rank[:, None, :], (NY, PIECE, TOK)).reshape(ROWS, TOK)
    gate_b = jnp.broadcast_to(gate_of[:, None, :], (NY, PIECE, TOK)).reshape(ROWS, TOK)
    slot = lax.rem(lax.broadcasted_iota(jnp.int32, (ROWS, TOK), 0), PIECE).astype(F32)
    for h in range(HALF):
        chosen = rank_b == slot + float(h * PIECE)
        one_hot = jnp.where(chosen, 1.0, 0.0).astype(BF16)
        sel[h * ROWS : (h + 1) * ROWS, :] = one_hot
        slot_gate = jnp.sum(jnp.where(chosen, gate_b, 0.0), axis=1, keepdims=True)
        picked = dot_nt(one_hot, pair)
        picked = jnp.where(upper, slot_gate * picked, picked)
        snd[h] = picked.astype(BF16).reshape(NY, PIECE, LANES)

    pl.semaphore_wait(barrier, len(partners))
    pl.semaphore_signal(by_two.at[0], inc=1, device_id=at_z(2), device_id_type=MESH)
    pl.semaphore_signal(by_two.at[1], inc=1, device_id=at_z(14), device_id_type=MESH)

    waits = []
    y_copies = [
        send(snd.at[:, lax.rem(y + d, NY)], rows.at[:, j, y], y_s.at[d - 1], y_r.at[d - 1], at_y(d))
        for d in Y_ORDER
    ]
    for h in range(HALF):
        rows[h, j, y] = snd[h, y]

    for load in loads[4:]:
        load.wait()
    zero_rows = jnp.zeros((LANES // 2 - COLS, HID), F32)

    def block(ref, num):
        first = num * COLS
        skip = first % 16
        return jnp.concatenate(
            [ref[first - skip : first + COLS, :].astype(F32)[skip:], zero_rows], axis=0
        ).astype(BF16)

    h0, h1 = slice(0, LANES), slice(LANES, HID)
    for num in range(8):
        low = slice(num * LANES, num * LANES + LANES // 2)
        high = slice(num * LANES + LANES // 2, (num + 1) * LANES)
        g_blk, u_blk, d_blk = block(wg, num), block(wu, num), block(wd, num)
        wp_gu[low, :] = jnp.concatenate([g_blk[:, h0], u_blk[:, h0], g_blk[:, h1], u_blk[:, h1]], axis=1)
        wp_gu[high, :] = jnp.zeros((LANES // 2, 2 * HID), BF16)
        wp_d[low, :] = jnp.zeros((LANES // 2, HID), BF16)
        wp_d[high, :] = d_blk

    for copy in y_copies:
        copy.wait_recv()
    waits += y_copies

    x_copies = []
    c_copies = []
    for h in range(HALF):
        mine = rows.at[h, j]
        x_copies.append({
            d: send(mine, mine, x_s.at[h, d - 1], x_r.at[h, d - 1], at_x(d)) for d in X_ORDER
        })
        c_copies.append({0: send(mine, mine, c_s.at[h, 0], c_r.at[h, 0], sib)})

    rn_copies = []
    for h in range(HALF):
        for d in X_ORDER:
            x_copies[h][d].wait_recv()
            piece = rows.at[h, lax.rem(x + NX - d, NX) * 2 + c]
            c_copies[h][d] = send(piece, piece, c_s.at[h, d], c_r.at[h, d], sib)
        acc_gu = jnp.zeros((ROWS, 2 * HID), F32)
        acc_d = jnp.zeros((ROWS, HID), F32)
        for d in (0,) + X_ORDER:
            c_copies[h][d].wait_recv()
            chip = lax.rem(x + NX - d, NX)
            lhs = jnp.concatenate(
                [rows[h, chip * 2].reshape(ROWS, LANES), rows[h, chip * 2 + 1].reshape(ROWS, LANES)], axis=1
            )
            span = pl.ds(pl.multiple_of(chip * 2 * LANES, 2 * LANES), 2 * LANES)
            acc_gu = acc_gu + dot(lhs, wp_gu[span, :])
            acc_d = acc_d + dot(lhs, wp_d[span, :])
        lo = jnp.concatenate([acc_gu[:, :HID], acc_d[:, :LANES]], axis=1).reshape(NZ, 8, 3 * LANES)
        hi = jnp.concatenate([acc_gu[:, HID:], acc_d[:, LANES:]], axis=1).reshape(NZ, 8, 3 * LANES)
        both = jnp.concatenate([lo, hi], axis=1).reshape(QUAD, QUAD, 16, 3 * LANES)
        part_f[h] = both
        part_b[h] = both.astype(BF16)
        rn_copies.append([
            [
                send(
                    part_b.at[h, lax.rem(z + d, QUAD), lax.rem(lax.rem(z + d, NZ) // QUAD + ahead, QUAD)],
                    near_r.at[h, num, k], rn_s.at[h, num, k], rn_r.at[h, num, k], at_z(d),
                )
                for num, d in enumerate(NEAR[h])
            ]
            for k, ahead in enumerate(AHEAD)
        ])
        if h == 0:
            pl.semaphore_wait(by_two.at[0], 1)
            pl.semaphore_wait(by_two.at[1], 1)
            pl.semaphore_signal(by_four, inc=1, device_id=at_z(4), device_id_type=MESH)
        waits += list(x_copies[h].values()) + list(c_copies[h].values())

    rf_copies = []
    own_sum = []
    for h in range(HALF):
        rf_copies.append([])
        for k, ahead in enumerate(AHEAD):
            piece = part_f[h, q, lax.rem(m + ahead, QUAD)]
            for num in range(QUAD - 1):
                rn_copies[h][k][num].wait_recv()
                piece = piece + near_r[h, num, k].astype(F32)
            waits += rn_copies[h][k]
            if ahead == 0:
                own_sum.append(piece)
                continue
            quad_b[h, k] = piece.astype(BF16)
            if h == 0 and k == 0:
                pl.semaphore_wait(by_four, 1)
            rf_copies[h].append(
                send(quad_b.at[h, k], far_r.at[h, k], rf_s.at[h, k], rf_r.at[h, k], at_z(FAR[k]))
            )

    for h in range(HALF):
        for num in range(8):
            rows_t[num * LANES : (num + 1) * LANES, h * ROWS : (h + 1) * ROWS] = (
                rows[h, num].reshape(ROWS, LANES).T
            )

    gf_copies = []
    gn_copies = []
    for h in range(HALF):
        total = own_sum[h]
        for num in range(QUAD - 1):
            rf_copies[h][num].wait_recv()
            total = total + far_r[h, num].astype(F32)
        pre_gate = total[:, :LANES]
        pre_up = total[:, LANES : 2 * LANES]
        back = total[:, 2 * LANES :]
        sigma = 1.0 / (1.0 + jnp.exp(-pre_gate))
        hidden = pre_gate * sigma * pre_up
        d_gate = back * pre_up * sigma * (1.0 + pre_gate * (1.0 - sigma))
        d_up = back * pre_gate * sigma
        hid_r[h, q, m] = jnp.concatenate([d_gate, d_up, hidden], axis=1).astype(BF16)
        mine = hid_r.at[h, q, m]
        gf_copies.append([
            send(mine, mine, gf_s.at[h, num], gf_r.at[h, num], at_z(d)) for num, d in enumerate(FAR)
        ])
        gn_copies.append([
            send(mine, mine, gn_s.at[h, 3, num], gn_r.at[h, 3, num], at_z(d)) for num, d in enumerate(NEAR[h])
        ])
        waits += rf_copies[h]

    for k, h in ((1, 0), (2, 0), (1, 1), (2, 1), (0, 0), (0, 1)):
        gf_copies[h][k].wait_recv()
        waits.append(gf_copies[h][k])
        piece = hid_r.at[h, q, lax.rem(m + QUAD - AHEAD[k], QUAD)]
        gn_copies[h] += [
            send(piece, piece, gn_s.at[h, k, num], gn_r.at[h, k, num], at_z(d)) for num, d in enumerate(NEAR[h])
        ]

    low_lane = lax.broadcasted_iota(jnp.int32, (ROWS // 2, LANES), 1) < LANES // 2
    e1_copies = []
    e2_copies = []

    def sum_cores(h):
        e1_copies[h].wait_recv()
        for chip in range(NX):
            total = ret[h, chip, c] + ret_sib[h, chip]
            ret_sum[h, chip] = total
            ret_send[h, chip] = total.astype(BF16)
        e2_copies.append([
            send(ret_send.at[h, lax.rem(x + d, NX)], ret_x.at[h, d - 1], e2_s.at[h, d - 1], e2_r.at[h, d - 1], at_x(d))
            for d in X_ORDER
        ])

    for h in range(HALF):
        for copy in gn_copies[h]:
            copy.wait_recv()
        waits += gn_copies[h]
        got = hid_r[h].reshape(NZ, 16, 3 * LANES).astype(F32)
        lo = got[:, :8].reshape(ROWS, 3 * LANES)
        hi = got[:, 8:].reshape(ROWS, 3 * LANES)
        d_gu = jnp.concatenate([lo[:, :HID], hi[:, :HID]], axis=1).astype(BF16)
        span = slice(h * ROWS, (h + 1) * ROWS)
        dgu[span, :] = d_gu
        hid[span, :] = jnp.concatenate([lo[:, HID:], hi[:, HID:]], axis=1).astype(BF16)
        for num in range(8):
            out = dot_nt(d_gu, wp_gu[num * LANES : (num + 1) * LANES, :])
            ret[h, num // 2, num % 2] = jnp.where(
                low_lane, out[: ROWS // 2], pltpu.roll(out[ROWS // 2 :], LANES // 2, 1)
            )
        e1_copies.append(send(ret.at[h, :, 1 - c], ret_sib.at[h], e1_s.at[h], e1_r.at[h], sib))
        if h == 0:
            sum_cores(0)
    sum_cores(1)
    waits += e1_copies

    gu_all = dgu[...]
    hid_all = hid[...]
    for num in range(8):
        low = slice(num * LANES, num * LANES + LANES // 2)
        high = slice(num * LANES + LANES // 2, (num + 1) * LANES)
        to = slice(num * COLS, (num + 1) * COLS)
        both = dot(rows_t[low, :], gu_all)[:COLS]
        og[to, h0] = both[:, :LANES]
        ou[to, h0] = both[:, LANES:HID]
        og[to, h1] = both[:, HID : HID + LANES]
        ou[to, h1] = both[:, HID + LANES :]
        od[to, :] = dot(rows_t[high, :], hid_all)[:COLS]
    stores = [
        pltpu.make_async_copy(src, dst.at[0, 0], out_sem.at[num])
        for num, (src, dst) in enumerate(((og, og_hbm), (ou, ou_hbm), (od, od_hbm)))
    ]
    for store in stores:
        store.start()

    ends = []
    for h in range(HALF):
        total = ret_sum[h, x]
        for d in X_ORDER:
            e2_copies[h][X_ORDER.index(d)].wait_recv()
            total = total + ret_x[h, d - 1].astype(F32)
        ends.append(total)
        waits += e2_copies[h]
    first = jnp.where(low_lane, ends[0], pltpu.roll(ends[1], LANES // 2, 1))
    second = jnp.where(low_lane, pltpu.roll(ends[0], LANES // 2, 1), ends[1])
    home_s[: NY // 2] = first.astype(BF16).reshape(NY // 2, PIECE, LANES)
    home_s[NY // 2 :] = second.astype(BF16).reshape(NY // 2, PIECE, LANES)
    f_copies = [
        send(home_s.at[lax.rem(y + d, NY)], home_r.at[y], f_s.at[d - 1], f_r.at[d - 1], at_y(d))
        for d in Y_ORDER
    ]
    home_r[y] = home_s[y]
    for copy in waits:
        copy.wait_send()
    for copy in f_copies:
        copy.wait_recv()
    home = home_r[...].reshape(ROWS, LANES).astype(F32).T
    both = jnp.concatenate([home[: LANES // 2], home[LANES // 2 :]], axis=1).astype(BF16)
    tok[...] = dot(both, sel[...])[:COLS].astype(BF16)
    last = pltpu.make_async_copy(tok, tok_out, out_sem.at[3])
    last.start()
    for copy in f_copies:
        copy.wait_send()
    for store in stores:
        store.wait()
    last.wait()


def hand_over(*refs):
    count = len(refs) // 2
    sems = refs[-1]
    copies = [pltpu.make_async_copy(refs[i], refs[count + i], sems.at[i]) for i in range(count)]
    for copy in copies:
        copy.start()
    for copy in copies:
        copy.wait()


def per_device(grad_out, tokens_in, expert_ids, gate_values, w_gate, w_up, w_down_t):
    vm = pltpu.VMEM
    dma = pltpu.SemaphoreType.DMA
    scratch = [
        vm((COLS, TOK), BF16), vm((COLS, TOK), BF16), vm((8, TOK), jnp.int32), vm((8, TOK), F32),
        vm((FEAT, HID), BF16), vm((FEAT, HID), BF16), vm((FEAT, HID), BF16),
        vm((HALF * ROWS, TOK), BF16),
        vm((HALF, NY, PIECE, LANES), BF16),
        vm((HALF, 8, NY, PIECE, LANES), BF16),
        vm((8 * LANES, 2 * HID), BF16),
        vm((8 * LANES, HID), BF16),
        vm((HALF, QUAD, QUAD, 16, 3 * LANES), F32),
        vm((HALF, QUAD, QUAD, 16, 3 * LANES), BF16),
        vm((HALF, QUAD - 1, QUAD, 16, 3 * LANES), BF16),
        vm((HALF, QUAD - 1, 16, 3 * LANES), BF16),
        vm((HALF, QUAD - 1, 16, 3 * LANES), BF16),
        vm((HALF, QUAD, QUAD, 16, 3 * LANES), BF16),
        vm((8 * LANES, HALF * ROWS), BF16),
        vm((HALF * ROWS, 2 * HID), BF16),
        vm((HALF * ROWS, HID), BF16),
        vm((HALF, NX, 2, ROWS // 2, LANES), F32),
        vm((HALF, NX, ROWS // 2, LANES), F32),
        vm((HALF, NX, ROWS // 2, LANES), F32),
        vm((HALF, NX, ROWS // 2, LANES), BF16),
        vm((HALF, NX - 1, ROWS // 2, LANES), BF16),
        vm((NY, PIECE, LANES), BF16),
        vm((NY, PIECE, LANES), BF16),
        vm((COLS, TOK), BF16),
        vm((FEAT, HID), F32), vm((FEAT, HID), F32), vm((FEAT, HID), F32),
        dma((7,)), dma((4,)),
        dma((NY - 1,)), dma((NY - 1,)),
        dma((HALF, NX - 1)), dma((HALF, NX - 1)),
        dma((HALF, NX)), dma((HALF, NX)),
        dma((HALF, QUAD - 1, QUAD)), dma((HALF, QUAD - 1, QUAD)),
        dma((HALF, QUAD - 1)), dma((HALF, QUAD - 1)),
        dma((HALF, QUAD - 1)), dma((HALF, QUAD - 1)),
        dma((HALF, QUAD, QUAD - 1)), dma((HALF, QUAD, QUAD - 1)),
        dma((HALF,)), dma((HALF,)),
        dma((HALF, NX - 1)), dma((HALF, NX - 1)),
        dma((NY - 1,)), dma((NY - 1,)),
        pltpu.SemaphoreType.REGULAR((2,)), pltpu.SemaphoreType.REGULAR,
    ]
    grad = jax.ShapeDtypeStruct((1, 1, FEAT, HID), F32)
    found = pl.pallas_call(
        kernel,
        name="expert_backward",
        out_shape=(jax.ShapeDtypeStruct((COLS, TOK), BF16), grad, grad, grad),
        in_specs=[pl.BlockSpec(memory_space=pltpu.HBM)] * 7,
        out_specs=[pl.BlockSpec(memory_space=pltpu.HBM)] * 4,
        scratch_shapes=scratch,
        compiler_params=pltpu.CompilerParams(
            collective_id=0, has_side_effects=True, vmem_limit_bytes=VMEM_FOR_KERNEL
        ),
    )(grad_out.T, tokens_in.T, expert_ids.T, gate_values.T, w_gate, w_up, w_down_t)
    tok_t, d_gate, d_up, d_down = pl.pallas_call(
        hand_over,
        name="hand_over",
        out_shape=[jax.ShapeDtypeStruct(each.shape, each.dtype) for each in found],
        in_specs=[pl.BlockSpec(memory_space=pltpu.VMEM)] * 4,
        out_specs=[pl.BlockSpec(memory_space=pl.ANY)] * 4,
        scratch_shapes=[dma((4,))],
    )(*found)
    return tok_t.T, d_gate, d_up, d_down


def solution(mesh):
    placed = (
        P("group", "local"),
        P("group", "local"),
        P("group", None),
        P("group", None),
        P("group", "local", None, None),
        P("group", "local", None, None),
        P("group", "local", None, None),
    )
    return jax.shard_map(
        per_device,
        mesh=mesh,
        in_specs=placed,
        out_specs=(
            P("group", "local"),
            P("group", "local", None, None),
            P("group", "local", None, None),
            P("group", "local", None, None),
        ),
        check_vma=False,
    )
```

```python
import jax
import jax.numpy as jnp
from jax import lax
from jax.experimental import pallas as pl
from jax.experimental.pallas import tpu as pltpu
from jax.sharding import PartitionSpec as P

EXP_GRP = 32
CAP = 32
NY = 8
NZ = 16
NX = 4
TOK = 512
COLS = 56
FEAT = 448
HID = 256
HALF = 2
ROWS = NY * CAP // HALF
PIECE = CAP // HALF
LANES = 128
MESH = pl.DeviceIdType.MESH
VMEM_FOR_KERNEL = (64 << 20) - 1441792
BF16 = jnp.bfloat16
F32 = jnp.float32
QUAD = 4
FAR = ((0, 8), (1, 12), (3, 4))
OWN = 2
CUTS = (slice(0, 1), slice(1, 4))
NEAR = ((2, 1, 15), (14, 1, 15))
Z_BESIDE = (2, 14, 1, 15)
Y_ORDER = (4, 3, 5, 2, 6, 1, 7)
Y_SPLIT = ((0, 1, 7, 2), (6, 3, 5, 4))
X_ORDER = (1, 3, 2)


def dot(left, right):
    return jnp.dot(left, right, preferred_element_type=F32)


def dot_nt(left, right):
    return lax.dot_general(left, right, (((1,), (1,)), ((), ())), preferred_element_type=F32)


def kernel(
    dy_hbm, x_hbm, ids_hbm, gate_hbm, wg_hbm, wu_hbm, wd_hbm,
    tok_out, og_hbm, ou_hbm, od_hbm,
    dy, xin, ids, gates, wg, wu, wd,
    sel, snd, rows, wp_gu, wp_d, part_f, part_b, near_r, quad_b, far_r, mine_r, near_g, spread, rows_t,
    dgu, hid, ret, ret_sib, ret_sum, ret_send, ret_x, home_s, home_r, tok, og, ou, od,
    in_sem, out_sem, y_s, y_r, x_s, x_r, c_s, c_r, rn_s, rn_r, rf_s, rf_r, gf_s, gf_r, gn_s, gn_r,
    e1_s, e1_r, e2_s, e2_r, f_s, f_r, by_two, by_four,
):
    y = lax.axis_index("group")
    l = lax.axis_index("local")
    z = l // 8
    q = lax.rem(z, QUAD)
    m = z // QUAD
    j = lax.rem(l, 8)
    x = j // 2
    c = lax.rem(j, 2)

    def at_y(d):
        return (lax.rem(y + d, NY), l)

    def at_z(d):
        return (y, lax.rem(z + d, NZ) * 8 + j)

    def at_x(d):
        return (y, z * 8 + lax.rem(x + d, NX) * 2 + c)

    sib = (y, z * 8 + x * 2 + 1 - c)

    barrier = pltpu.get_barrier_semaphore()
    partners = (
        [at_z(d) for d in Z_BESIDE] + [at_y(d) for d in Y_ORDER] + [at_x(d) for d in X_ORDER] + [sib]
    )
    for who in partners:
        pl.semaphore_signal(barrier, inc=1, device_id=who, device_id_type=MESH)

    loads = [
        pltpu.make_async_copy(src, dst, in_sem.at[num])
        for num, (src, dst) in enumerate(
            (
                (ids_hbm, ids),
                (gate_hbm, gates),
                (x_hbm, xin),
                (dy_hbm, dy),
                (wg_hbm.at[0, 0], wg),
                (wu_hbm.at[0, 0], wu),
                (wd_hbm.at[0, 0], wd),
            )
        )
    ]
    for load in loads:
        load.start()

    def send(src, dst, send_sem, recv_sem, who):
        copy = pltpu.make_async_remote_copy(
            src_ref=src, dst_ref=dst, send_sem=send_sem, recv_sem=recv_sem,
            device_id=who, device_id_type=MESH,
        )
        copy.start()
        return copy

    loads[0].wait()
    loads[1].wait()
    ids_t = ids[...]
    gates_t = gates[...]
    target = lax.broadcasted_iota(jnp.int32, (NY, TOK), 0) * EXP_GRP
    hit = jnp.zeros((NY, TOK), F32)
    gate_of = jnp.zeros((NY, TOK), F32)
    for k in range(8):
        same = jnp.broadcast_to(ids_t[k : k + 1], (NY, TOK)) == target
        hit = jnp.where(same, 1.0, hit)
        gate_of = gate_of + jnp.where(same, jnp.broadcast_to(gates_t[k : k + 1], (NY, TOK)), 0.0)
    before = (
        lax.broadcasted_iota(jnp.int32, (TOK, TOK), 0) < lax.broadcasted_iota(jnp.int32, (TOK, TOK), 1)
    )
    rank = dot(hit.astype(BF16), jnp.where(before, 1.0, 0.0).astype(BF16))
    rank = jnp.where(hit > 0.0, rank, -1.0)
    loads[2].wait()
    loads[3].wait()
    gap = jnp.zeros((LANES // 2 - COLS, TOK), F32)
    pair = jnp.concatenate([xin[...].astype(F32), gap, dy[...].astype(F32), gap], axis=0).astype(BF16)
    upper = lax.broadcasted_iota(jnp.int32, (ROWS, LANES), 1) >= LANES // 2
    rank_b = jnp.broadcast_to(rank[:, None, :], (NY, PIECE, TOK)).reshape(ROWS, TOK)
    gate_b = jnp.broadcast_to(gate_of[:, None, :], (NY, PIECE, TOK)).reshape(ROWS, TOK)
    slot = lax.rem(lax.broadcasted_iota(jnp.int32, (ROWS, TOK), 0), PIECE).astype(F32)
    for h in range(HALF):
        chosen = rank_b == slot + float(h * PIECE)
        one_hot = jnp.where(chosen, 1.0, 0.0).astype(BF16)
        sel[h * ROWS : (h + 1) * ROWS, :] = one_hot
        slot_gate = jnp.sum(jnp.where(chosen, gate_b, 0.0), axis=1, keepdims=True)
        picked = dot_nt(one_hot, pair)
        picked = jnp.where(upper, slot_gate * picked, picked)
        snd[:, h * PIECE : (h + 1) * PIECE] = picked.astype(BF16).reshape(NY, PIECE, LANES)

    pl.semaphore_wait(barrier, len(partners))
    pl.semaphore_signal(by_two.at[0], inc=1, device_id=at_z(2), device_id_type=MESH)
    pl.semaphore_signal(by_two.at[1], inc=1, device_id=at_z(14), device_id_type=MESH)

    waits = []
    y_copies = {}
    for d in Y_ORDER:
        h = 0 if d in Y_SPLIT[0] else 1
        y_copies[d] = send(
            snd.at[lax.rem(y + d, NY)], rows.at[h, j, Y_SPLIT[h].index(d)], y_s.at[d - 1], y_r.at[d - 1], at_y(d)
        )
    rows[0, j, 0] = snd[y]

    for load in loads[4:]:
        load.wait()
    zero_rows = jnp.zeros((LANES // 2 - COLS, HID), F32)

    def block(ref, num):
        first = num * COLS
        skip = first % 16
        return jnp.concatenate(
            [ref[first - skip : first + COLS, :].astype(F32)[skip:], zero_rows], axis=0
        ).astype(BF16)

    h0, h1 = slice(0, LANES), slice(LANES, HID)
    for num in range(8):
        low = slice(num * LANES, num * LANES + LANES // 2)
        high = slice(num * LANES + LANES // 2, (num + 1) * LANES)
        g_blk, u_blk, d_blk = block(wg, num), block(wu, num), block(wd, num)
        wp_gu[low, :] = jnp.concatenate([g_blk[:, h0], u_blk[:, h0], g_blk[:, h1], u_blk[:, h1]], axis=1)
        wp_gu[high, :] = jnp.zeros((LANES // 2, 2 * HID), BF16)
        wp_d[low, :] = jnp.zeros((LANES // 2, HID), BF16)
        wp_d[high, :] = d_blk

    x_copies = []
    c_copies = []
    for h in range(HALF):
        for d in Y_SPLIT[h]:
            if d > 0:
                y_copies[d].wait_recv()
        mine = rows.at[h, j]
        x_copies.append({
            d: send(mine, mine, x_s.at[h, d - 1], x_r.at[h, d - 1], at_x(d)) for d in X_ORDER
        })
        c_copies.append({0: send(mine, mine, c_s.at[h, 0], c_r.at[h, 0], sib)})
    waits += list(y_copies.values())
    for h in range(HALF):
        for d in X_ORDER:
            x_copies[h][d].wait_recv()
            piece = rows.at[h, lax.rem(x + NX - d, NX) * 2 + c]
            c_copies[h][d] = send(piece, piece, c_s.at[h, d], c_r.at[h, d], sib)

    rn_copies = []
    for h in range(HALF):
        acc_gu = jnp.zeros((ROWS, 2 * HID), F32)
        acc_d = jnp.zeros((ROWS, HID), F32)
        for d in (0,) + X_ORDER:
            c_copies[h][d].wait_recv()
            chip = lax.rem(x + NX - d, NX)
            lhs = jnp.concatenate(
                [rows[h, chip * 2].reshape(ROWS, LANES), rows[h, chip * 2 + 1].reshape(ROWS, LANES)], axis=1
            )
            span = pl.ds(pl.multiple_of(chip * 2 * LANES, 2 * LANES), 2 * LANES)
            acc_gu = acc_gu + dot(lhs, wp_gu[span, :])
            acc_d = acc_d + dot(lhs, wp_d[span, :])
        lo = jnp.concatenate([acc_gu[:, :HID], acc_d[:, :LANES]], axis=1).reshape(NZ, 8, 3 * LANES)
        hi = jnp.concatenate([acc_gu[:, HID:], acc_d[:, LANES:]], axis=1).reshape(NZ, 8, 3 * LANES)
        both = jnp.concatenate([lo, hi], axis=1).reshape(QUAD, QUAD, 16, 3 * LANES)
        for num in range(QUAD):
            apart = lax.rem(num + QUAD - q, QUAD)
            step = jnp.where(apart == 3, NZ - 1, jnp.where(apart == 2, NEAR[h][0], apart))
            lead = lax.rem(z + step, NZ) // QUAD
            for part in range(QUAD):
                place = lax.rem(part + 2 * QUAD - lead + 2, QUAD)
                part_f[h, num, place] = both[num, part]
                part_b[h, num, place] = both[num, part].astype(BF16)
        rn_copies.append([
            [
                send(
                    part_b.at[h, lax.rem(z + d, QUAD), cut], near_r.at[h, num, cut],
                    rn_s.at[h, num, k], rn_r.at[h, num, k], at_z(d),
                )
                for num, d in enumerate(NEAR[h])
            ]
            for k, cut in enumerate(CUTS)
        ])
        if h == 0:
            pl.semaphore_wait(by_two.at[0], 1)
            pl.semaphore_wait(by_two.at[1], 1)
            pl.semaphore_signal(by_four, inc=1, device_id=at_z(4), device_id_type=MESH)
        waits += list(x_copies[h].values()) + list(c_copies[h].values())

    rf_copies = []
    own_sum = []
    for k, cut in enumerate(CUTS):
        for h in range(HALF):
            total = part_f[h, q, cut]
            for num in range(QUAD - 1):
                rn_copies[h][k][num].wait_recv()
                total = total + near_r[h, num, cut].astype(F32)
            waits += rn_copies[h][k]
            if k == 0:
                rf_copies.append({})
            else:
                own_sum.append(total[OWN - cut.start])
            quad_b[h, cut] = total.astype(BF16)
            if h == 0 and k == 0:
                pl.semaphore_wait(by_four, 1)
            for place, d in FAR:
                if cut.start <= place < cut.stop:
                    rf_copies[h][place] = send(
                        quad_b.at[h, place], far_r.at[h, place], rf_s.at[h, place], rf_r.at[h, place], at_z(d)
                    )

    for h in range(HALF):
        for num in range(8):
            rows_t[num * LANES : (num + 1) * LANES, h * ROWS : (h + 1) * ROWS] = (
                rows[h, num].reshape(ROWS, LANES).T
            )

    gf_copies = []
    gn_copies = []
    for h in range(HALF):
        total = own_sum[h]
        for place, d in reversed(FAR):
            rf_copies[h][place].wait_recv()
            total = total + far_r[h, place].astype(F32)
        pre_gate = total[:, :LANES]
        pre_up = total[:, LANES : 2 * LANES]
        back = total[:, 2 * LANES :]
        sigma = 1.0 / (1.0 + jnp.exp(-pre_gate))
        hidden = pre_gate * sigma * pre_up
        d_gate = back * pre_up * sigma * (1.0 + pre_gate * (1.0 - sigma))
        d_up = back * pre_gate * sigma
        mine_r[h, OWN] = jnp.concatenate([d_gate, d_up, hidden], axis=1).astype(BF16)
        gf_copies.append({
            place: send(mine_r.at[h, OWN], mine_r.at[h, place], gf_s.at[h, place], gf_r.at[h, place], at_z(NZ - d))
            for place, d in FAR
        })
        waits += list(rf_copies[h].values())

    for k in (1, 0):
        for h in range(HALF):
            for place, d in FAR:
                if CUTS[k].start <= place < CUTS[k].stop:
                    gf_copies[h][place].wait_recv()
            if k == 1:
                waits += list(gf_copies[h].values())
                gn_copies.append([])
            gn_copies[h] += [
                send(
                    mine_r.at[h, CUTS[k]], near_g.at[h, num, CUTS[k]], gn_s.at[h, num, k], gn_r.at[h, num, k], at_z(d)
                )
                for num, d in enumerate(NEAR[h])
            ]

    low_lane = lax.broadcasted_iota(jnp.int32, (ROWS // 2, LANES), 1) < LANES // 2
    e1_copies = []
    e2_copies = []

    def sum_cores(h):
        e1_copies[h].wait_recv()
        for chip in range(NX):
            total = ret[h, chip, c] + ret_sib[h, chip]
            ret_sum[h, chip] = total
            ret_send[h, chip] = total.astype(BF16)
        e2_copies.append([
            send(ret_send.at[h, lax.rem(x + d, NX)], ret_x.at[h, d - 1], e2_s.at[h, d - 1], e2_r.at[h, d - 1], at_x(d))
            for d in X_ORDER
        ])

    for h in range(HALF):
        for copy in gn_copies[h]:
            copy.wait_recv()
        waits += gn_copies[h]
        for num in range(QUAD):
            owner = z if num == QUAD - 1 else lax.rem(z + NZ - NEAR[h][num], NZ)
            for place in range(QUAD):
                got = (mine_r[h, place] if num == QUAD - 1 else near_g[h, num, place]).astype(F32)
                rank_of = lax.rem(owner, QUAD) * QUAD + lax.rem(owner // QUAD + place + 2, QUAD)
                spread[h, rank_of] = jnp.concatenate([got[:8], got[8:]], axis=1)
        whole = spread[h].reshape(ROWS, 6 * LANES)
        lo = whole[:, : 3 * LANES]
        hi = whole[:, 3 * LANES :]
        d_gu = jnp.concatenate([lo[:, :HID], hi[:, :HID]], axis=1).astype(BF16)
        span = slice(h * ROWS, (h + 1) * ROWS)
        dgu[span, :] = d_gu
        hid[span, :] = jnp.concatenate([lo[:, HID:], hi[:, HID:]], axis=1).astype(BF16)
        for num in range(8):
            out = dot_nt(d_gu, wp_gu[num * LANES : (num + 1) * LANES, :])
            ret[h, num // 2, num % 2] = jnp.where(
                low_lane, out[: ROWS // 2], pltpu.roll(out[ROWS // 2 :], LANES // 2, 1)
            )
        e1_copies.append(send(ret.at[h, :, 1 - c], ret_sib.at[h], e1_s.at[h], e1_r.at[h], sib))
    sum_cores(0)
    sum_cores(1)
    waits += e1_copies

    f_copies = []
    low_piece = lax.broadcasted_iota(jnp.int32, (PIECE, LANES), 1) < LANES // 2

    def return_rows(h):
        total = ret_sum[h, x]
        for num, d in enumerate(X_ORDER):
            e2_copies[h][num].wait_recv()
            total = total + ret_x[h, d - 1].astype(F32)
        turned = pltpu.roll(total, LANES // 2, 1)
        for num, d in enumerate(Y_SPLIT[h]):
            first = CAP * (num % 2)
            one = slice(first, first + PIECE)
            two = slice(first + PIECE, first + CAP)
            if num < 2:
                block_out = jnp.where(low_piece, total[one], turned[two])
            else:
                block_out = jnp.where(low_piece, turned[one], total[two])
            home_s[h, num] = block_out.astype(BF16)
            if d == 0:
                home_r[y] = home_s[h, num]
            else:
                f_copies.append(
                    send(home_s.at[h, num], home_r.at[y], f_s.at[d - 1], f_r.at[d - 1], at_y(NY - d))
                )

    return_rows(0)

    return_rows(1)
    for h in range(HALF):
        waits += e2_copies[h]
    gu_all = dgu[...]
    hid_all = hid[...]
    for num in range(8):
        low = slice(num * LANES, num * LANES + LANES // 2)
        high = slice(num * LANES + LANES // 2, (num + 1) * LANES)
        to = slice(num * COLS, (num + 1) * COLS)
        both = dot(rows_t[low, :], gu_all)[:COLS]
        og[to, h0] = both[:, :LANES]
        ou[to, h0] = both[:, LANES:HID]
        og[to, h1] = both[:, HID : HID + LANES]
        ou[to, h1] = both[:, HID + LANES :]
        od[to, :] = dot(rows_t[high, :], hid_all)[:COLS]
    stores = [
        pltpu.make_async_copy(src, dst.at[0, 0], out_sem.at[num])
        for num, (src, dst) in enumerate(((og, og_hbm), (ou, ou_hbm), (od, od_hbm)))
    ]
    for store in stores:
        store.start()

    for copy in waits:
        copy.wait_send()
    for copy in f_copies:
        copy.wait_recv()
    home = home_r[...].reshape(ROWS, LANES).astype(F32).T
    both = jnp.concatenate([home[: LANES // 2], home[LANES // 2 :]], axis=1).astype(BF16)
    tok[...] = dot(both, sel[...])[:COLS].astype(BF16)
    last = pltpu.make_async_copy(tok, tok_out, out_sem.at[3])
    last.start()
    for copy in f_copies:
        copy.wait_send()
    for store in stores:
        store.wait()
    last.wait()


def hand_over(*refs):
    found, given, held, sems = refs[:4], refs[4:8], refs[8:12], refs[12]
    loads = [pltpu.make_async_copy(found[i], held[i], sems.at[0, i]) for i in range(4)]
    stores = [pltpu.make_async_copy(held[i], given[i], sems.at[1, i]) for i in range(4)]
    for load in loads:
        load.start()
    for load, store in zip(loads, stores):
        load.wait()
        store.start()
    for store in stores:
        store.wait()


def per_device(grad_out, tokens_in, expert_ids, gate_values, w_gate, w_up, w_down_t):
    vm = pltpu.VMEM
    dma = pltpu.SemaphoreType.DMA
    scratch = [
        vm((COLS, TOK), BF16), vm((COLS, TOK), BF16), vm((8, TOK), jnp.int32), vm((8, TOK), F32),
        vm((FEAT, HID), BF16), vm((FEAT, HID), BF16), vm((FEAT, HID), BF16),
        vm((HALF * ROWS, TOK), BF16),
        vm((NY, CAP, LANES), BF16),
        vm((HALF, 8, NY // 2, CAP, LANES), BF16),
        vm((8 * LANES, 2 * HID), BF16),
        vm((8 * LANES, HID), BF16),
        vm((HALF, QUAD, QUAD, 16, 3 * LANES), F32),
        vm((HALF, QUAD, QUAD, 16, 3 * LANES), BF16),
        vm((HALF, QUAD - 1, QUAD, 16, 3 * LANES), BF16),
        vm((HALF, QUAD, 16, 3 * LANES), BF16),
        vm((HALF, QUAD, 16, 3 * LANES), BF16),
        vm((HALF, QUAD, 16, 3 * LANES), BF16),
        vm((HALF, QUAD - 1, QUAD, 16, 3 * LANES), BF16),
        vm((HALF, NZ, 8, 6 * LANES), F32),
        vm((8 * LANES, HALF * ROWS), BF16),
        vm((HALF * ROWS, 2 * HID), BF16),
        vm((HALF * ROWS, HID), BF16),
        vm((HALF, NX, 2, ROWS // 2, LANES), F32),
        vm((HALF, NX, ROWS // 2, LANES), F32),
        vm((HALF, NX, ROWS // 2, LANES), F32),
        vm((HALF, NX, ROWS // 2, LANES), BF16),
        vm((HALF, NX - 1, ROWS // 2, LANES), BF16),
        vm((HALF, NY // 2, PIECE, LANES), BF16),
        vm((NY, PIECE, LANES), BF16),
        vm((COLS, TOK), BF16),
        vm((FEAT, HID), F32), vm((FEAT, HID), F32), vm((FEAT, HID), F32),
        dma((7,)), dma((4,)),
        dma((NY - 1,)), dma((NY - 1,)),
        dma((HALF, NX - 1)), dma((HALF, NX - 1)),
        dma((HALF, NX)), dma((HALF, NX)),
        dma((HALF, QUAD - 1, 2)), dma((HALF, QUAD - 1, 2)),
        dma((HALF, QUAD)), dma((HALF, QUAD)),
        dma((HALF, QUAD)), dma((HALF, QUAD)),
        dma((HALF, QUAD - 1, 2)), dma((HALF, QUAD - 1, 2)),
        dma((HALF,)), dma((HALF,)),
        dma((HALF, NX - 1)), dma((HALF, NX - 1)),
        dma((NY - 1,)), dma((NY - 1,)),
        pltpu.SemaphoreType.REGULAR((2,)), pltpu.SemaphoreType.REGULAR,
    ]
    grad = jax.ShapeDtypeStruct((1, 1, FEAT, HID), F32)
    found = pl.pallas_call(
        kernel,
        name="expert_backward",
        out_shape=(jax.ShapeDtypeStruct((COLS, TOK), BF16), grad, grad, grad),
        in_specs=[pl.BlockSpec(memory_space=pltpu.HBM)] * 7,
        out_specs=[pl.BlockSpec(memory_space=pltpu.HBM)] * 4,
        scratch_shapes=scratch,
        compiler_params=pltpu.CompilerParams(
            collective_id=0, has_side_effects=True, vmem_limit_bytes=VMEM_FOR_KERNEL
        ),
    )(grad_out.T, tokens_in.T, expert_ids.T, gate_values.T, w_gate, w_up, w_down_t)
    tok_t, d_gate, d_up, d_down = pl.pallas_call(
        hand_over,
        name="hand_over",
        out_shape=[jax.ShapeDtypeStruct(each.shape, each.dtype) for each in found],
        in_specs=[pl.BlockSpec(memory_space=pl.ANY)] * 4,
        out_specs=[pl.BlockSpec(memory_space=pl.ANY)] * 4,
        scratch_shapes=[vm(each.shape, each.dtype) for each in found] + [dma((2, 4))],
    )(*found)
    return tok_t.T, d_gate, d_up, d_down


def solution(mesh):
    placed = (
        P("group", "local"),
        P("group", "local"),
        P("group", None),
        P("group", None),
        P("group", "local", None, None),
        P("group", "local", None, None),
        P("group", "local", None, None),
    )
    return jax.shard_map(
        per_device,
        mesh=mesh,
        in_specs=placed,
        out_specs=(
            P("group", "local"),
            P("group", "local", None, None),
            P("group", "local", None, None),
            P("group", "local", None, None),
        ),
        check_vma=False,
    )
```

```python
import jax
import jax.numpy as jnp
from jax import lax
from jax.experimental import pallas as pl
from jax.experimental.pallas import tpu as pltpu
from jax.sharding import PartitionSpec as P

EXP_GRP = 32
CAP = 32
NY = 8
NZ = 16
NX = 4
TOK = 512
COLS = 56
FEAT = 448
HID = 256
HALF = 2
ROWS = NY * CAP // HALF
PIECE = CAP // HALF
LANES = 128
MESH = pl.DeviceIdType.MESH
VMEM_FOR_KERNEL = (64 << 20) - 1441792
BF16 = jnp.bfloat16
F32 = jnp.float32
QUAD = 4
FAR = ((0, 8), (1, 12), (3, 4))
OWN = 2
CUTS = (slice(0, 1), slice(1, 4))
NEAR = ((2, 1, 15), (14, 1, 15))
Z_BESIDE = (2, 14, 1, 15)
Y_ORDER = (4, 3, 5, 2, 6, 1, 7)
Y_SPLIT = ((0, 1, 7, 2), (6, 3, 5, 4))
X_ORDER = (1, 3, 2)


def dot(left, right):
    return jnp.dot(left, right, preferred_element_type=F32)


def dot_nt(left, right):
    return lax.dot_general(left, right, (((1,), (1,)), ((), ())), preferred_element_type=F32)


def kernel(
    dy_hbm, x_hbm, ids_hbm, gate_hbm, wg_hbm, wu_hbm, wd_hbm,
    home_r, sel_hbm, og_hbm, ou_hbm, od_hbm,
    dy, xin, ids, gates, wg, wu, wd,
    sel, snd, rows, wp_gu, wp_d, part_f, part_b, near_r, quad_b, far_r, mine_r, near_g, spread, rows_t,
    dgu, hid, ret, ret_sib, ret_sum, ret_send, ret_x, home_s, og, ou, od,
    in_sem, out_sem, y_s, y_r, x_s, x_r, c_s, c_r, rn_s, rn_r, rf_s, rf_r, gf_s, gf_r, gn_s, gn_r,
    e1_s, e1_r, e2_s, e2_r, f_s, f_r, by_two, by_four,
):
    y = lax.axis_index("group")
    l = lax.axis_index("local")
    z = l // 8
    q = lax.rem(z, QUAD)
    m = z // QUAD
    j = lax.rem(l, 8)
    x = j // 2
    c = lax.rem(j, 2)

    def at_y(d):
        return (lax.rem(y + d, NY), l)

    def at_z(d):
        return (y, lax.rem(z + d, NZ) * 8 + j)

    def at_x(d):
        return (y, z * 8 + lax.rem(x + d, NX) * 2 + c)

    sib = (y, z * 8 + x * 2 + 1 - c)

    barrier = pltpu.get_barrier_semaphore()
    partners = (
        [at_z(d) for d in Z_BESIDE] + [at_y(d) for d in Y_ORDER] + [at_x(d) for d in X_ORDER] + [sib]
    )
    for who in partners:
        pl.semaphore_signal(barrier, inc=1, device_id=who, device_id_type=MESH)

    loads = [
        pltpu.make_async_copy(src, dst, in_sem.at[num])
        for num, (src, dst) in enumerate(
            (
                (ids_hbm, ids),
                (gate_hbm, gates),
                (x_hbm, xin),
                (dy_hbm, dy),
                (wg_hbm.at[0, 0], wg),
                (wu_hbm.at[0, 0], wu),
                (wd_hbm.at[0, 0], wd),
            )
        )
    ]
    for load in loads:
        load.start()

    def send(src, dst, send_sem, recv_sem, who):
        copy = pltpu.make_async_remote_copy(
            src_ref=src, dst_ref=dst, send_sem=send_sem, recv_sem=recv_sem,
            device_id=who, device_id_type=MESH,
        )
        copy.start()
        return copy

    loads[0].wait()
    loads[1].wait()
    ids_t = ids[...]
    gates_t = gates[...]
    target = lax.broadcasted_iota(jnp.int32, (NY, TOK), 0) * EXP_GRP
    hit = jnp.zeros((NY, TOK), F32)
    gate_of = jnp.zeros((NY, TOK), F32)
    for k in range(8):
        same = jnp.broadcast_to(ids_t[k : k + 1], (NY, TOK)) == target
        hit = jnp.where(same, 1.0, hit)
        gate_of = gate_of + jnp.where(same, jnp.broadcast_to(gates_t[k : k + 1], (NY, TOK)), 0.0)
    before = (
        lax.broadcasted_iota(jnp.int32, (TOK, TOK), 0) < lax.broadcasted_iota(jnp.int32, (TOK, TOK), 1)
    )
    rank = dot(hit.astype(BF16), jnp.where(before, 1.0, 0.0).astype(BF16))
    rank = jnp.where(hit > 0.0, rank, -1.0)
    loads[2].wait()
    loads[3].wait()
    gap = jnp.zeros((LANES // 2 - COLS, TOK), F32)
    pair = jnp.concatenate([xin[...].astype(F32), gap, dy[...].astype(F32), gap], axis=0).astype(BF16)
    upper = lax.broadcasted_iota(jnp.int32, (ROWS, LANES), 1) >= LANES // 2
    rank_b = jnp.broadcast_to(rank[:, None, :], (NY, PIECE, TOK)).reshape(ROWS, TOK)
    gate_b = jnp.broadcast_to(gate_of[:, None, :], (NY, PIECE, TOK)).reshape(ROWS, TOK)
    slot = lax.rem(lax.broadcasted_iota(jnp.int32, (ROWS, TOK), 0), PIECE).astype(F32)
    for h in range(HALF):
        chosen = rank_b == slot + float(h * PIECE)
        one_hot = jnp.where(chosen, 1.0, 0.0).astype(BF16)
        sel[h * ROWS : (h + 1) * ROWS, :] = one_hot
        slot_gate = jnp.sum(jnp.where(chosen, gate_b, 0.0), axis=1, keepdims=True)
        picked = dot_nt(one_hot, pair)
        picked = jnp.where(upper, slot_gate * picked, picked)
        snd[:, h * PIECE : (h + 1) * PIECE] = picked.astype(BF16).reshape(NY, PIECE, LANES)

    keep_sel = pltpu.make_async_copy(sel, sel_hbm, out_sem.at[3])
    keep_sel.start()
    pl.semaphore_wait(barrier, len(partners))
    pl.semaphore_signal(by_two.at[0], inc=1, device_id=at_z(2), device_id_type=MESH)
    pl.semaphore_signal(by_two.at[1], inc=1, device_id=at_z(14), device_id_type=MESH)

    waits = []
    y_copies = {}
    for d in Y_ORDER:
        h = 0 if d in Y_SPLIT[0] else 1
        y_copies[d] = send(
            snd.at[lax.rem(y + d, NY)], rows.at[h, j, Y_SPLIT[h].index(d)], y_s.at[d - 1], y_r.at[d - 1], at_y(d)
        )
    rows[0, j, 0] = snd[y]

    for load in loads[4:]:
        load.wait()
    zero_rows = jnp.zeros((LANES // 2 - COLS, HID), F32)

    def block(ref, num):
        first = num * COLS
        skip = first % 16
        return jnp.concatenate(
            [ref[first - skip : first + COLS, :].astype(F32)[skip:], zero_rows], axis=0
        ).astype(BF16)

    h0, h1 = slice(0, LANES), slice(LANES, HID)
    for num in range(8):
        low = slice(num * LANES, num * LANES + LANES // 2)
        high = slice(num * LANES + LANES // 2, (num + 1) * LANES)
        g_blk, u_blk, d_blk = block(wg, num), block(wu, num), block(wd, num)
        wp_gu[low, :] = jnp.concatenate([g_blk[:, h0], u_blk[:, h0], g_blk[:, h1], u_blk[:, h1]], axis=1)
        wp_gu[high, :] = jnp.zeros((LANES // 2, 2 * HID), BF16)
        wp_d[low, :] = jnp.zeros((LANES // 2, HID), BF16)
        wp_d[high, :] = d_blk

    x_copies = []
    c_copies = []
    for h in range(HALF):
        for d in Y_SPLIT[h]:
            if d > 0:
                y_copies[d].wait_recv()
        mine = rows.at[h, j]
        x_copies.append({
            d: send(mine, mine, x_s.at[h, d - 1], x_r.at[h, d - 1], at_x(d)) for d in X_ORDER
        })
        c_copies.append({0: send(mine, mine, c_s.at[h, 0], c_r.at[h, 0], sib)})
    waits += list(y_copies.values())
    for h in range(HALF):
        for d in X_ORDER:
            x_copies[h][d].wait_recv()
            piece = rows.at[h, lax.rem(x + NX - d, NX) * 2 + c]
            c_copies[h][d] = send(piece, piece, c_s.at[h, d], c_r.at[h, d], sib)

    rn_copies = []
    for h in range(HALF):
        acc_gu = jnp.zeros((ROWS, 2 * HID), F32)
        acc_d = jnp.zeros((ROWS, HID), F32)
        for d in (0,) + X_ORDER:
            c_copies[h][d].wait_recv()
            chip = lax.rem(x + NX - d, NX)
            lhs = jnp.concatenate(
                [rows[h, chip * 2].reshape(ROWS, LANES), rows[h, chip * 2 + 1].reshape(ROWS, LANES)], axis=1
            )
            span = pl.ds(pl.multiple_of(chip * 2 * LANES, 2 * LANES), 2 * LANES)
            acc_gu = acc_gu + dot(lhs, wp_gu[span, :])
            acc_d = acc_d + dot(lhs, wp_d[span, :])
        lo = jnp.concatenate([acc_gu[:, :HID], acc_d[:, :LANES]], axis=1).reshape(NZ, 8, 3 * LANES)
        hi = jnp.concatenate([acc_gu[:, HID:], acc_d[:, LANES:]], axis=1).reshape(NZ, 8, 3 * LANES)
        both = jnp.concatenate([lo, hi], axis=1).reshape(QUAD, QUAD, 16, 3 * LANES)
        for num in range(QUAD):
            apart = lax.rem(num + QUAD - q, QUAD)
            step = jnp.where(apart == 3, NZ - 1, jnp.where(apart == 2, NEAR[h][0], apart))
            lead = lax.rem(z + step, NZ) // QUAD
            for part in range(QUAD):
                place = lax.rem(part + 2 * QUAD - lead + 2, QUAD)
                part_f[h, num, place] = both[num, part]
                part_b[h, num, place] = both[num, part].astype(BF16)
        rn_copies.append([
            [
                send(
                    part_b.at[h, lax.rem(z + d, QUAD), cut], near_r.at[h, num, cut],
                    rn_s.at[h, num, k], rn_r.at[h, num, k], at_z(d),
                )
                for num, d in enumerate(NEAR[h])
            ]
            for k, cut in enumerate(CUTS)
        ])
        if h == 0:
            pl.semaphore_wait(by_two.at[0], 1)
            pl.semaphore_wait(by_two.at[1], 1)
            pl.semaphore_signal(by_four, inc=1, device_id=at_z(4), device_id_type=MESH)
        waits += list(x_copies[h].values()) + list(c_copies[h].values())

    rf_copies = []
    own_sum = []
    for k, cut in enumerate(CUTS):
        for h in range(HALF):
            total = part_f[h, q, cut]
            for num in range(QUAD - 1):
                rn_copies[h][k][num].wait_recv()
                total = total + near_r[h, num, cut].astype(F32)
            waits += rn_copies[h][k]
            if k == 0:
                rf_copies.append({})
            else:
                own_sum.append(total[OWN - cut.start])
            quad_b[h, cut] = total.astype(BF16)
            if h == 0 and k == 0:
                pl.semaphore_wait(by_four, 1)
            for place, d in FAR:
                if cut.start <= place < cut.stop:
                    rf_copies[h][place] = send(
                        quad_b.at[h, place], far_r.at[h, place], rf_s.at[h, place], rf_r.at[h, place], at_z(d)
                    )

    for h in range(HALF):
        for num in range(8):
            rows_t[num * LANES : (num + 1) * LANES, h * ROWS : (h + 1) * ROWS] = (
                rows[h, num].reshape(ROWS, LANES).T
            )

    gf_copies = []
    gn_copies = []
    for h in range(HALF):
        total = own_sum[h]
        for place, d in reversed(FAR):
            rf_copies[h][place].wait_recv()
            total = total + far_r[h, place].astype(F32)
        pre_gate = total[:, :LANES]
        pre_up = total[:, LANES : 2 * LANES]
        back = total[:, 2 * LANES :]
        sigma = 1.0 / (1.0 + jnp.exp(-pre_gate))
        hidden = pre_gate * sigma * pre_up
        d_gate = back * pre_up * sigma * (1.0 + pre_gate * (1.0 - sigma))
        d_up = back * pre_gate * sigma
        mine_r[h, OWN] = jnp.concatenate([d_gate, d_up, hidden], axis=1).astype(BF16)
        gf_copies.append({
            place: send(mine_r.at[h, OWN], mine_r.at[h, place], gf_s.at[h, place], gf_r.at[h, place], at_z(NZ - d))
            for place, d in FAR
        })
        waits += list(rf_copies[h].values())

    for k in (1, 0):
        for h in range(HALF):
            for place, d in FAR:
                if CUTS[k].start <= place < CUTS[k].stop:
                    gf_copies[h][place].wait_recv()
            if k == 1:
                waits += list(gf_copies[h].values())
                gn_copies.append([])
            gn_copies[h] += [
                send(
                    mine_r.at[h, CUTS[k]], near_g.at[h, num, CUTS[k]], gn_s.at[h, num, k], gn_r.at[h, num, k], at_z(d)
                )
                for num, d in enumerate(NEAR[h])
            ]

    low_lane = lax.broadcasted_iota(jnp.int32, (ROWS // 2, LANES), 1) < LANES // 2
    e1_copies = []
    e2_copies = []

    def sum_cores(h):
        e1_copies[h].wait_recv()
        for chip in range(NX):
            total = ret[h, chip, c] + ret_sib[h, chip]
            ret_sum[h, chip] = total
            ret_send[h, chip] = total.astype(BF16)
        e2_copies.append([
            send(ret_send.at[h, lax.rem(x + d, NX)], ret_x.at[h, d - 1], e2_s.at[h, d - 1], e2_r.at[h, d - 1], at_x(d))
            for d in X_ORDER
        ])

    for h in range(HALF):
        for copy in gn_copies[h]:
            copy.wait_recv()
        waits += gn_copies[h]
        for num in range(QUAD):
            owner = z if num == QUAD - 1 else lax.rem(z + NZ - NEAR[h][num], NZ)
            for place in range(QUAD):
                got = (mine_r[h, place] if num == QUAD - 1 else near_g[h, num, place]).astype(F32)
                rank_of = lax.rem(owner, QUAD) * QUAD + lax.rem(owner // QUAD + place + 2, QUAD)
                spread[h, rank_of] = jnp.concatenate([got[:8], got[8:]], axis=1)
        whole = spread[h].reshape(ROWS, 6 * LANES)
        lo = whole[:, : 3 * LANES]
        hi = whole[:, 3 * LANES :]
        d_gu = jnp.concatenate([lo[:, :HID], hi[:, :HID]], axis=1).astype(BF16)
        span = slice(h * ROWS, (h + 1) * ROWS)
        dgu[span, :] = d_gu
        hid[span, :] = jnp.concatenate([lo[:, HID:], hi[:, HID:]], axis=1).astype(BF16)
        for num in range(8):
            out = dot_nt(d_gu, wp_gu[num * LANES : (num + 1) * LANES, :])
            ret[h, num // 2, num % 2] = jnp.where(
                low_lane, out[: ROWS // 2], pltpu.roll(out[ROWS // 2 :], LANES // 2, 1)
            )
        e1_copies.append(send(ret.at[h, :, 1 - c], ret_sib.at[h], e1_s.at[h], e1_r.at[h], sib))
    sum_cores(0)
    sum_cores(1)
    waits += e1_copies

    f_copies = []
    own_rows = []
    low_piece = lax.broadcasted_iota(jnp.int32, (PIECE, LANES), 1) < LANES // 2

    def return_rows(h):
        total = ret_sum[h, x]
        for num, d in enumerate(X_ORDER):
            e2_copies[h][num].wait_recv()
            total = total + ret_x[h, d - 1].astype(F32)
        turned = pltpu.roll(total, LANES // 2, 1)
        for num, d in enumerate(Y_SPLIT[h]):
            first = CAP * (num % 2)
            one = slice(first, first + PIECE)
            two = slice(first + PIECE, first + CAP)
            if num < 2:
                block_out = jnp.where(low_piece, total[one], turned[two])
            else:
                block_out = jnp.where(low_piece, turned[one], total[two])
            home_s[h, num] = block_out.astype(BF16)
            if d == 0:
                own_rows.append(pltpu.make_async_copy(home_s.at[h, num], home_r.at[y], out_sem.at[4]))
                own_rows[0].start()
            else:
                f_copies.append(
                    send(home_s.at[h, num], home_r.at[y], f_s.at[d - 1], f_r.at[d - 1], at_y(NY - d))
                )

    return_rows(0)

    return_rows(1)
    for h in range(HALF):
        waits += e2_copies[h]
    gu_all = dgu[...]
    hid_all = hid[...]
    for num in range(8):
        low = slice(num * LANES, num * LANES + LANES // 2)
        high = slice(num * LANES + LANES // 2, (num + 1) * LANES)
        to = slice(num * COLS, (num + 1) * COLS)
        both = dot(rows_t[low, :], gu_all)[:COLS]
        og[to, h0] = both[:, :LANES]
        ou[to, h0] = both[:, LANES:HID]
        og[to, h1] = both[:, HID : HID + LANES]
        ou[to, h1] = both[:, HID + LANES :]
        od[to, :] = dot(rows_t[high, :], hid_all)[:COLS]
    stores = [
        pltpu.make_async_copy(src, dst.at[0, 0], out_sem.at[num])
        for num, (src, dst) in enumerate(((og, og_hbm), (ou, ou_hbm), (od, od_hbm)))
    ]
    for store in stores:
        store.start()

    for copy in waits:
        copy.wait_send()
    for copy in f_copies:
        copy.wait_recv()
    for copy in f_copies:
        copy.wait_send()
    for store in stores:
        store.wait()
    keep_sel.wait()
    own_rows[0].wait()


def scatter_rows(
    home_hbm, sel_hbm, og_hbm, ou_hbm, od_hbm, tok_out, og_out, ou_out, od_out, home_r, sel, og, ou, od, tok, sems
):
    loads = [
        pltpu.make_async_copy(src, dst, sems.at[0, num])
        for num, (src, dst) in enumerate(
            ((home_hbm, home_r), (sel_hbm, sel), (og_hbm, og), (ou_hbm, ou), (od_hbm, od))
        )
    ]
    stores = [
        pltpu.make_async_copy(src, dst, sems.at[1, num])
        for num, (src, dst) in enumerate(((tok, tok_out), (og, og_out), (ou, ou_out), (od, od_out)))
    ]
    for load in loads:
        load.start()
    loads[0].wait()
    loads[1].wait()
    home = home_r[...].reshape(ROWS, LANES).astype(F32).T
    both = jnp.concatenate([home[: LANES // 2], home[LANES // 2 :]], axis=1).astype(BF16)
    tok[...] = dot(both, sel[...])[:COLS].astype(BF16)
    stores[0].start()
    for load, store in zip(loads[2:], stores[1:]):
        load.wait()
        store.start()
    for store in stores:
        store.wait()


def per_device(grad_out, tokens_in, expert_ids, gate_values, w_gate, w_up, w_down_t):
    vm = pltpu.VMEM
    dma = pltpu.SemaphoreType.DMA
    scratch = [
        vm((COLS, TOK), BF16), vm((COLS, TOK), BF16), vm((8, TOK), jnp.int32), vm((8, TOK), F32),
        vm((FEAT, HID), BF16), vm((FEAT, HID), BF16), vm((FEAT, HID), BF16),
        vm((HALF * ROWS, TOK), BF16),
        vm((NY, CAP, LANES), BF16),
        vm((HALF, 8, NY // 2, CAP, LANES), BF16),
        vm((8 * LANES, 2 * HID), BF16),
        vm((8 * LANES, HID), BF16),
        vm((HALF, QUAD, QUAD, 16, 3 * LANES), F32),
        vm((HALF, QUAD, QUAD, 16, 3 * LANES), BF16),
        vm((HALF, QUAD - 1, QUAD, 16, 3 * LANES), BF16),
        vm((HALF, QUAD, 16, 3 * LANES), BF16),
        vm((HALF, QUAD, 16, 3 * LANES), BF16),
        vm((HALF, QUAD, 16, 3 * LANES), BF16),
        vm((HALF, QUAD - 1, QUAD, 16, 3 * LANES), BF16),
        vm((HALF, NZ, 8, 6 * LANES), F32),
        vm((8 * LANES, HALF * ROWS), BF16),
        vm((HALF * ROWS, 2 * HID), BF16),
        vm((HALF * ROWS, HID), BF16),
        vm((HALF, NX, 2, ROWS // 2, LANES), F32),
        vm((HALF, NX, ROWS // 2, LANES), F32),
        vm((HALF, NX, ROWS // 2, LANES), F32),
        vm((HALF, NX, ROWS // 2, LANES), BF16),
        vm((HALF, NX - 1, ROWS // 2, LANES), BF16),
        vm((HALF, NY // 2, PIECE, LANES), BF16),
        vm((FEAT, HID), F32), vm((FEAT, HID), F32), vm((FEAT, HID), F32),
        dma((7,)), dma((5,)),
        dma((NY - 1,)), dma((NY - 1,)),
        dma((HALF, NX - 1)), dma((HALF, NX - 1)),
        dma((HALF, NX)), dma((HALF, NX)),
        dma((HALF, QUAD - 1, 2)), dma((HALF, QUAD - 1, 2)),
        dma((HALF, QUAD)), dma((HALF, QUAD)),
        dma((HALF, QUAD)), dma((HALF, QUAD)),
        dma((HALF, QUAD - 1, 2)), dma((HALF, QUAD - 1, 2)),
        dma((HALF,)), dma((HALF,)),
        dma((HALF, NX - 1)), dma((HALF, NX - 1)),
        dma((NY - 1,)), dma((NY - 1,)),
        pltpu.SemaphoreType.REGULAR((2,)), pltpu.SemaphoreType.REGULAR,
    ]
    grad = jax.ShapeDtypeStruct((1, 1, FEAT, HID), F32)
    found = pl.pallas_call(
        kernel,
        name="expert_backward",
        out_shape=(
            jax.ShapeDtypeStruct((NY, PIECE, LANES), BF16),
            jax.ShapeDtypeStruct((HALF * ROWS, TOK), BF16),
            grad,
            grad,
            grad,
        ),
        in_specs=[pl.BlockSpec(memory_space=pltpu.HBM)] * 7,
        out_specs=[pl.BlockSpec(memory_space=pltpu.HBM)] * 5,
        scratch_shapes=scratch,
        compiler_params=pltpu.CompilerParams(
            collective_id=0, has_side_effects=True, vmem_limit_bytes=VMEM_FOR_KERNEL
        ),
    )(grad_out.T, tokens_in.T, expert_ids.T, gate_values.T, w_gate, w_up, w_down_t)
    tok_t, d_gate, d_up, d_down = pl.pallas_call(
        scatter_rows,
        name="scatter_rows",
        out_shape=[jax.ShapeDtypeStruct((COLS, TOK), BF16), grad, grad, grad],
        in_specs=[pl.BlockSpec(memory_space=pl.ANY)] * 5,
        out_specs=[pl.BlockSpec(memory_space=pl.ANY)] * 4,
        scratch_shapes=[vm(each.shape, each.dtype) for each in found] + [vm((COLS, TOK), BF16), dma((2, 5))],
    )(*found)
    return tok_t.T, d_gate, d_up, d_down


def solution(mesh):
    placed = (
        P("group", "local"),
        P("group", "local"),
        P("group", None),
        P("group", None),
        P("group", "local", None, None),
        P("group", "local", None, None),
        P("group", "local", None, None),
    )
    return jax.shard_map(
        per_device,
        mesh=mesh,
        in_specs=placed,
        out_specs=(
            P("group", "local"),
            P("group", "local", None, None),
            P("group", "local", None, None),
            P("group", "local", None, None),
        ),
        check_vma=False,
    )
```
